512 devices in a mesh: group: 8 (over y_lo, core), blk: 64 (over x, z, y_hi).
Axes of the slice: x: 4, y: 8 (y_hi: 2, y_lo: 4; y = y_hi * 4 + y_lo), z: 8, core: 2. Of those that a mesh axis runs over, the one named last changes fastest.
Arguments:
- picture_vectors: bfloat16 [65536, 1152], P(('group', 'blk')), may hold values from -1 to 1
- caption_vectors: bfloat16 [65536, 1152], P(('group', 'blk')), may hold values from -1 to 1
- inverse_heat_factor: float32 [1], replicated, may hold values from 0.5 to 2
- score_shift_term: float32 [1], replicated, may hold values from -3 to 1
Outputs:
- grad_images: float32 [65536, 1152], P(('group', 'blk'))
- grad_texts: float32 [65536, 1152], P(('group', 'blk'))
- row_loss: float32 [65536], P(('group', 'blk'))
The draws below stay inside these ranges and needn't reach their ends.
All inputs are finite; a program needn't handle non-finite values.
Results may differ from the reference program's by a relative error of at most 0.015.
Values may be sent and summed in bfloat16 or wider, within the bound.
No kernel may reach another device: no remote copies, remote signals or barrier semaphores. Data moves between devices by JAX's collectives and lax.ppermute only.
A program may use at most 64 MiB of HBM per device.

```python
import math
import jax
import jax.numpy as jnp
from jax import lax

D = 1152
ROWS = 128
SPAN = 2
BUNDLE = 1024
TOKENS = 65536
N_GROUP = 8
N_BLK = 64


def block_scale(stream_key, extent, pieces, least, top_value):
    factor_of, own = 1.0, jax.random.fold_in(stream_key, 6)
    for position, parts in pieces:
        heights = jnp.exp(jax.random.uniform(jax.random.fold_in(own, position), (parts,), jnp.float32, least / len(pieces), top_value / len(pieces)))
        factor_of = factor_of * jnp.repeat(heights, extent[position] // parts).reshape([-1 if axis == position else 1 for axis in range(len(extent))])
    return factor_of


def centred(key, dims, width, bound, cuts=(), dtype=jnp.bfloat16):
    values = width * jax.random.normal(key, dims, jnp.float32)
    if cuts:
        values = values * block_scale(key, dims, cuts, -0.22, 0.18)
    return jnp.clip(values, -bound, bound).astype(dtype)


def setup_inputs(seed: int = 0) -> dict:
    splits = jax.random.split(jax.random.key(seed), 5)
    picture_vectors = centred(splits[0], (TOKENS, D), 0.171, 1.0, ((0, 512),))
    caption_vectors = centred(splits[1], (TOKENS, D), 0.171, 1.0, ((0, 512),))
    inverse_heat_factor = jnp.clip(jnp.exp(jax.random.uniform(splits[2], (1,), jnp.float32, math.log(0.5), math.log(2.0))), 0.5, 2.0)
    score_shift_term = jnp.clip(jax.random.uniform(splits[3], (1,), jnp.float32, -3.0, 1.0), -3.0, 1.0)
    return {"picture_vectors": picture_vectors, "caption_vectors": caption_vectors, "inverse_heat_factor": inverse_heat_factor, "score_shift_term": score_shift_term}


def reference(picture_vectors, caption_vectors, inverse_heat_factor, score_shift_term):
    group_width = N_GROUP
    cycle_size = N_BLK
    image_four = picture_vectors.reshape(group_width, cycle_size, ROWS, D).astype(jnp.float32)
    text_quad_block = caption_vectors.reshape(group_width, cycle_size, ROWS, D)
    score_multiplier = inverse_heat_factor[0]
    shift_value = score_shift_term[0]
    bundles = []
    for step in range(SPAN):
        rolled = jnp.roll(text_quad_block, step, axis=1)
        bundles.append(rolled.transpose(1, 0, 2, 3).reshape(cycle_size, BUNDLE, D).astype(jnp.float32))
    loss_rows = []
    image_rows = []
    text_total = jnp.zeros((cycle_size, BUNDLE, D), jnp.float32)
    for group_id in range(group_width):
        images_here = image_four[group_id]
        positives = jnp.arange(BUNDLE)[None, :] == (group_id * ROWS + jnp.arange(ROWS)[:, None])
        positives = positives[None, :, :]
        loss_sum = jnp.zeros((cycle_size, ROWS), jnp.float32)
        grad_image = jnp.zeros((cycle_size, ROWS, D), jnp.float32)
        group_part = jnp.zeros((cycle_size, BUNDLE, D), jnp.float32)
        for step in range(SPAN):
            text_bundle = bundles[step]
            logits = jnp.einsum("brd,bhd->brh", images_here, text_bundle)
            scaled = score_multiplier * logits + shift_value
            if step == 0:
                signs = jnp.where(positives, 1.0, -1.0).astype(jnp.float32) * jnp.ones_like(scaled)
            else:
                signs = -jnp.ones_like(scaled)
            loss_sum = loss_sum + jnp.sum(jax.nn.softplus(-signs * scaled), axis=-1)
            slopes = (-signs * jax.nn.sigmoid(-signs * scaled) * score_multiplier).astype(jnp.bfloat16).astype(jnp.float32)
            grad_image = grad_image + jnp.einsum("brh,bhd->brd", slopes, text_bundle)
            grad_bundle = jnp.einsum("brh,brd->bhd", slopes, images_here)
            group_part = group_part + jnp.roll(grad_bundle, -step, axis=0)
        rounded = lax.optimization_barrier(group_part.astype(jnp.bfloat16))
        text_total = text_total + rounded.astype(jnp.float32)
        loss_rows.append(loss_sum)
        image_rows.append(grad_image)
    grad_text = text_total.reshape(cycle_size, group_width, ROWS, D).transpose(1, 0, 2, 3)
    loss_all = jnp.stack(loss_rows, axis=0)
    grad_image_all = jnp.stack(image_rows, axis=0)
    row_loss = (loss_all / (SPAN * BUNDLE)).reshape(TOKENS)
    return grad_image_all.reshape(TOKENS, D), grad_text.reshape(TOKENS, D), row_loss
```

```python
import jax
import jax.numpy as jnp
import numpy as np
from jax import lax
from jax.sharding import Mesh, PartitionSpec as P

AXES = ("yl", "c", "x", "z", "yh")
BF = jnp.bfloat16
F32 = jnp.float32


def pairs(sizes, fn):
    out = []
    for src in np.ndindex(*sizes):
        out.append((int(np.ravel_multi_index(src, sizes)), int(np.ravel_multi_index(fn(*src), sizes))))
    return out


def visit(sizes):
    nyl, _, nx, nz, _ = sizes

    def fn(yl, c, x, z, yh):
        if yh == 1:
            return nyl - 1 - yl, c, x, z, 0
        k = (x * nz + z - 1) % (nx * nz)
        return nyl - 1 - yl, c, k // nz, k % nz, 1

    return pairs(sizes, fn)


def other_core(sizes):
    return pairs(sizes, lambda yl, c, x, z, yh: (yl, 1 - c, x, z, yh))


def contract(left, right, dims):
    return lax.dot_general(left, right, (dims, ((), ())), preferred_element_type=F32)


def split16(v):
    hi = v.astype(BF)
    return hi, (v - hi.astype(F32)).astype(BF)


def pack(rows, values):
    hi, lo = split16(values)
    n, width = values.shape[0], rows.shape[1]
    extra = jnp.zeros((16, width), BF).at[0, :n].set(hi).at[1, :n].set(lo)
    return jnp.concatenate([rows, extra], axis=0)


def unpack(message, n):
    m = message.shape[0] - 16
    values = message[m, :n].astype(F32) + message[m + 1, :n].astype(F32)
    return message[:m].astype(F32), values


def solution(mesh):
    sizes = (4, 2, 4, 8, 2)
    fine = Mesh(mesh.devices.reshape(sizes), AXES)
    go = visit(sizes)
    back = [(b, a) for a, b in go]
    swap = other_core(sizes)

    def shards(images, texts, scale, shift):
        rows, width = images.shape
        yl, c = lax.axis_index("yl"), lax.axis_index("c")
        s, b = scale[0], shift[0]
        visitors = lax.ppermute(images, AXES, go)
        spread = jnp.broadcast_to(texts[None], (4, rows, width))
        bundle = lax.all_to_all(spread, "yl", 0, 0).reshape(4 * rows, width)
        mine = lax.all_gather(images, "c", axis=0, tiled=True)
        theirs = lax.all_gather(visitors, "c", axis=0, tiled=True)
        everyone = jnp.concatenate([mine, theirs], axis=0)
        z = s * contract(everyone, bundle, ((1,), (1,))) + b
        i = lax.broadcasted_iota(jnp.int32, z.shape, 0)
        j = lax.broadcasted_iota(jnp.int32, z.shape, 1)
        positive = (i - c * rows == j - yl * rows) & (i >= c * rows) & (i < (c + 1) * rows)
        u = jnp.where(positive, -z, z)
        e = jnp.exp(-jnp.abs(u))
        loss = jnp.sum(jnp.maximum(u, 0.0) + jnp.log1p(e), axis=1)
        sig = jnp.where(u >= 0, 1.0, e) / (1.0 + e)
        slopes = (jnp.where(positive, -s, s) * sig).astype(BF)
        grad_all = contract(slopes, bundle, ((1,), (0,))).reshape(2, 2, rows, width)
        loss_all = loss.reshape(2, 2, rows)
        keep = lax.dynamic_index_in_dim(grad_all, c, 1, keepdims=False)
        give = lax.dynamic_index_in_dim(grad_all, 1 - c, 1, keepdims=False)
        keep_loss = lax.dynamic_index_in_dim(loss_all, c, 1, keepdims=False)
        give_loss = lax.dynamic_index_in_dim(loss_all, 1 - c, 1, keepdims=False)
        got, got_loss = unpack(
            lax.ppermute(pack(give.reshape(2 * rows, width).astype(BF), give_loss.reshape(-1)), AXES, swap),
            2 * rows,
        )
        grad = keep + got.reshape(2, rows, width)
        loss2 = keep_loss + got_loss.reshape(2, rows)
        home, home_loss = unpack(
            lax.ppermute(pack(grad[1].astype(BF), loss2[1]), AXES, back), rows
        )
        part = contract(slopes, everyone, ((0,), (0,))).astype(BF).reshape(4, rows, width)
        parts = lax.all_to_all(part, "yl", 0, 0)
        grad_texts = jnp.sum(parts.astype(F32), axis=0)
        grad_images = grad[0] + home
        row_loss = (loss2[0] + home_loss) / (16 * rows)
        return grad_images, grad_texts, row_loss

    whole = P(AXES, None)
    return jax.shard_map(
        shards,
        mesh=fine,
        in_specs=(whole, whole, P(), P()),
        out_specs=(whole, whole, P(AXES)),
        check_vma=False,
    )
```

```python
import functools

import jax
import jax.numpy as jnp
import numpy as np
from jax import lax
from jax.experimental import pallas as pl
from jax.experimental.pallas import tpu as pltpu
from jax.sharding import Mesh, PartitionSpec as P

AXES = ("yl", "c", "x", "z", "yh")
BF = jnp.bfloat16
F32 = jnp.float32
EXTRA = 16


def pairs(sizes, fn):
    out = []
    for src in np.ndindex(*sizes):
        out.append((int(np.ravel_multi_index(src, sizes)), int(np.ravel_multi_index(fn(*src), sizes))))
    return out


def visit(sizes):
    nyl, _, nx, nz, _ = sizes

    def fn(yl, c, x, z, yh):
        if yh == 1:
            return nyl - 1 - yl, c, x, z, 0
        k = (x * nz + z - 1) % (nx * nz)
        return nyl - 1 - yl, c, k // nz, k % nz, 1

    return pairs(sizes, fn)


def along_line(sizes, m):
    return pairs(sizes, lambda yl, c, x, z, yh: (yl ^ m, c, x, z, yh))


def contract(left, right, dims):
    return lax.dot_general(left, right, (dims, ((), ())), preferred_element_type=F32)


def slopes_and_loss(positive, factors, images, texts, slopes, loss):
    s, b = factors[0], factors[1]
    z = s * contract(texts[...], images[...], ((1,), (1,))) + b
    pair = positive(z.shape) if positive else None
    u = z if pair is None else jnp.where(pair, -z, z)
    e = jnp.exp(-jnp.abs(u))
    loss[...] = jnp.sum(jnp.maximum(u, 0.0) + jnp.log1p(e), axis=0, keepdims=True)
    slope = s * jnp.where(u >= 0, 1.0, e) / (1.0 + e)
    slopes[...] = (slope if pair is None else jnp.where(pair, -slope, slope)).astype(BF)


def lay(blocks, bundle):
    rows = blocks[0].shape[0]
    for m, block in enumerate(blocks):
        bundle[m * rows : (m + 1) * rows, :] = block[...]


def own_kernel(place, factors, mine, own, far, cross, slopes, loss, bundle):
    lay((own, far, cross), bundle)
    rows = own.shape[0]

    def positive(shape):
        i = lax.broadcasted_iota(jnp.int32, shape, 1) - place[0] * rows
        j = lax.broadcasted_iota(jnp.int32, shape, 0)
        return (i == j) & (j < rows)

    slopes_and_loss(positive, factors, mine, bundle, slopes, loss)


def far_kernel(factors, mine, theirs, own, far, my_slopes, slopes, loss, far_grad, bundle):
    lay((own, far), bundle)
    slopes_and_loss(None, factors, theirs, bundle, slopes, loss)
    rows = own.shape[0]
    far_grad[...] = (
        contract(my_slopes[rows : 2 * rows, :], mine[...], ((1,), (0,)))
        + contract(slopes[rows:, :], theirs[...], ((1,), (0,)))
    ).astype(BF)


def extra_rows(values, width):
    n = values.shape[1]
    hi = values.astype(BF).astype(F32)
    lo = (values - hi).astype(BF).astype(F32)
    row = lax.broadcasted_iota(jnp.int32, (EXTRA, n), 0)
    head = jnp.where(row == 0, hi, jnp.where(row == 1, lo, 0.0))
    return jnp.concatenate([head, jnp.zeros((EXTRA, width - n), F32)], axis=1).astype(BF)


def split_cores(core, total, summed, keep, keep_loss, give):
    rows = keep.shape[0]
    at = pl.multiple_of(core * rows, rows)
    away = pl.multiple_of((1 - core) * rows, rows)
    keep[...] = total[pl.ds(at, rows), :]
    give[:rows, :] = total[pl.ds(away, rows), :].astype(BF)
    zero, one = summed[:, :rows], summed[:, rows:]
    keep_loss[...] = jnp.where(core == 0, zero, one)
    give[rows:, :] = extra_rows(jnp.where(core == 0, one, zero), give.shape[1])


def visit_kernel(
    place, factors, mine, theirs, own, far, near, cross, first_slopes, first_loss, my_loss,
    slopes, near_slopes, loss, keep, keep_loss, give, total, first, second, their_loss,
):
    lay((own, far), first)
    lay((near, cross), second)
    slopes_and_loss(None, factors, theirs, second, slopes, their_loss)
    slopes_and_loss(None, factors, mine, near, near_slopes, loss)
    loss[...] += my_loss[...]
    total[...] = contract(first_slopes[...], first[...], ((0,), (0,))) + contract(
        slopes[...], second[...], ((0,), (0,))
    )
    split_cores(place[0], total, their_loss[...] + first_loss[...], keep, keep_loss, give)


def rest_kernel(
    place, mine, theirs, own, far, near, cross, my_slopes, near_slopes, first_slopes, slopes, loss, after,
    own_grad, near_grad, cross_grad, keep, keep_loss, give, total, bundle,
):
    rows = own.shape[0]

    def text_gradient(of_mine, of_theirs):
        return contract(of_mine, mine[...], ((1,), (0,))) + contract(of_theirs, theirs[...], ((1,), (0,)))

    own_grad[...] = text_gradient(my_slopes[:rows, :], first_slopes[:rows, :])
    near_grad[...] = text_gradient(near_slopes[...], slopes[:rows, :]).astype(BF)
    cross_grad[...] = text_gradient(my_slopes[2 * rows :, :], slopes[rows:, :]).astype(BF)
    lay((own, far, cross), bundle)
    total[...] = contract(my_slopes[...], bundle[...], ((0,), (0,))) + contract(
        near_slopes[...], near[...], ((0,), (0,))
    )
    split_cores(place[0], total, loss[...], keep, keep_loss, give)


def take(place, gathered, rows):
    size = rows + EXTRA
    at = pl.multiple_of((1 - place[0]) * size, size)
    got = gathered[pl.ds(at, rows), :].astype(F32)
    extra = gathered[pl.ds(pl.multiple_of(at + rows, EXTRA), EXTRA), :].astype(F32)
    return got, extra[0:1, :rows] + extra[1:2, :rows]


def visitor_kernel(place, keep, keep_loss, gathered, message):
    rows = keep.shape[0]
    got, got_loss = take(place, gathered, rows)
    message[:rows, :] = (keep[...] + got).astype(BF)
    message[rows:, :] = extra_rows(keep_loss[...] + got_loss, keep.shape[1])


def image_kernel(place, keep, keep_loss, gathered, home, grad, loss):
    rows = keep.shape[0]
    got, got_loss = take(place, gathered, rows)
    grad[...] = keep[...] + got + home[:rows, :].astype(F32)
    extra = home[rows:, :].astype(F32)
    loss[...] = (keep_loss[...] + got_loss + extra[0:1, :rows] + extra[1:2, :rows]) * (1.0 / (16 * rows))


SMEM = pl.BlockSpec(memory_space=pltpu.SMEM)
VMEM = pl.BlockSpec(memory_space=pltpu.VMEM)


def call(kernel, scalars, outs, scratch=()):
    def run(*args):
        return pl.pallas_call(
            kernel,
            out_shape=outs,
            in_specs=[SMEM] * scalars + [VMEM] * (len(args) - scalars),
            out_specs=[VMEM] * len(outs),
            scratch_shapes=list(scratch),
            compiler_params=pltpu.CompilerParams(vmem_limit_bytes=32 * 1024 * 1024),
            cost_estimate=pl.CostEstimate(flops=0, bytes_accessed=0, transcendentals=0),
        )(*args)

    return run


def solution(mesh):
    sizes = (4, 2, 4, 8, 2)
    fine = Mesh(mesh.devices.reshape(sizes), AXES)
    go = visit(sizes)
    back = [(b, a) for a, b in go]
    bar = lax.optimization_barrier
    across = [along_line(sizes, m) for m in range(sizes[0])]

    def shards(images, texts, scale, shift):
        rows, width = images.shape
        shape = jax.ShapeDtypeStruct
        place = lax.axis_index("c").reshape(1).astype(jnp.int32)
        factors = jnp.concatenate([scale, shift])
        block, wide = shape((rows, width), BF), shape((rows, width), F32)
        short, message = shape((1, rows), F32), shape((rows + EXTRA, width), BF)
        line = shape((1, 2 * rows), F32)
        total = pltpu.VMEM((2 * rows, width), F32)

        def slope(blocks):
            return shape((blocks * rows, 2 * rows), BF)

        def bundle(blocks):
            return pltpu.VMEM((blocks * rows, width), BF)

        def both_cores(array):
            return lax.all_gather(array, "c", axis=0, tiled=True)

        far, cross, near = (lax.ppermute(texts, AXES, across[m]) for m in (2, 3, 1))
        visitors = lax.ppermute(images, AXES, go)
        mine = both_cores(images)

        my_slopes, my_loss = call(own_kernel, 2, [slope(3), line], [bundle(3)])(
            place, factors, mine, texts, far, cross
        )
        visitors, my_slopes = bar((visitors, my_slopes))
        theirs = both_cores(visitors)
        slopes0, loss0, far_grad = call(far_kernel, 1, [slope(2), line, block], [bundle(2)])(
            factors, mine, theirs, texts, far, my_slopes
        )
        far_home = lax.ppermute(far_grad, AXES, across[2])
        slopes1, near_slopes, loss, keep_v, keep_loss_v, give_v = call(
            visit_kernel,
            2,
            [slope(2), slope(1), line, wide, short, message],
            [total, bundle(2), bundle(2), pltpu.VMEM((1, 2 * rows), F32)],
        )(place, factors, mine, theirs, texts, far, near, cross, slopes0, loss0, my_loss)
        (sent,) = call(visitor_kernel, 1, [message])(place, keep_v, keep_loss_v, both_cores(give_v))
        home = lax.ppermute(sent, AXES, back)
        own_grad, near_grad, cross_grad, keep, keep_loss, give = call(
            rest_kernel, 1, [wide, block, block, wide, short, message], [total, bundle(3)]
        )(place, mine, theirs, texts, far, near, cross, my_slopes, near_slopes, slopes0, slopes1, loss, sent)
        cross_home = lax.ppermute(cross_grad, AXES, across[3])
        near_home = lax.ppermute(near_grad, AXES, across[1])

        two = own_grad + far_home.astype(F32)
        keep, two = bar((keep, two))
        grad_images, row_loss = call(image_kernel, 1, [wide, short])(
            place, keep, keep_loss, both_cores(give), home
        )
        grad_images, row_loss, two = bar((grad_images, row_loss, two))
        grad_texts = two + (cross_home.astype(F32) + near_home.astype(F32))
        row_loss = row_loss.reshape(rows)
        return grad_images, grad_texts, row_loss

    whole = P(AXES, None)
    return jax.shard_map(
        shards,
        mesh=fine,
        in_specs=(whole, whole, P(), P()),
        out_specs=(whole, whole, P(AXES)),
        check_vma=False,
    )
```

```python
import functools

import jax
import jax.numpy as jnp
import numpy as np
from jax import lax
from jax.experimental import pallas as pl
from jax.experimental.pallas import tpu as pltpu
from jax.sharding import Mesh, PartitionSpec as P

AXES = ("yl", "c", "x", "z", "yh")
BF = jnp.bfloat16
F32 = jnp.float32
EXTRA = 16


def pairs(sizes, fn):
    out = []
    for src in np.ndindex(*sizes):
        out.append((int(np.ravel_multi_index(src, sizes)), int(np.ravel_multi_index(fn(*src), sizes))))
    return out


def visit(sizes):
    nyl, _, nx, nz, _ = sizes

    def fn(yl, c, x, z, yh):
        if yh == 1:
            return nyl - 1 - yl, c, x, z, 0
        k = (x * nz + z - 1) % (nx * nz)
        return nyl - 1 - yl, c, k // nz, k % nz, 1

    return pairs(sizes, fn)


def along_line(sizes, m):
    return pairs(sizes, lambda yl, c, x, z, yh: (yl ^ m, c, x, z, yh))


def contract(left, right, dims):
    return lax.dot_general(left, right, (dims, ((), ())), preferred_element_type=F32)


def slopes_and_loss(positive, factors, images, texts, slopes, loss):
    s, b = factors[0], factors[1]
    z = s * contract(texts[...], images[...], ((1,), (1,))) + b
    pair = positive(z.shape) if positive else None
    u = z if pair is None else jnp.where(pair, -z, z)
    e = jnp.exp(-jnp.abs(u))
    loss[...] = jnp.sum(jnp.maximum(u, 0.0) + jnp.log1p(e), axis=0, keepdims=True)
    slope = s * jnp.where(u >= 0, 1.0, e) / (1.0 + e)
    slopes[...] = (slope if pair is None else jnp.where(pair, -slope, slope)).astype(BF)


def lay(blocks, bundle):
    rows = blocks[0].shape[0]
    for m, block in enumerate(blocks):
        bundle[m * rows : (m + 1) * rows, :] = block[...]


def own_kernel(place, factors, mine, own, cross, near, slopes, loss, bundle):
    lay((own, cross, near), bundle)
    rows = own.shape[0]

    def positive(shape):
        i = lax.broadcasted_iota(jnp.int32, shape, 1) - place[0] * rows
        j = lax.broadcasted_iota(jnp.int32, shape, 0)
        return (i == j) & (j < rows)

    slopes_and_loss(positive, factors, mine, bundle, slopes, loss)


def cross_kernel(factors, mine, theirs, own, cross, my_slopes, slopes, loss, cross_grad, bundle):
    lay((own, cross), bundle)
    slopes_and_loss(None, factors, theirs, bundle, slopes, loss)
    rows = own.shape[0]
    cross_grad[...] = (
        contract(my_slopes[rows : 2 * rows, :], mine[...], ((1,), (0,)))
        + contract(slopes[rows:, :], theirs[...], ((1,), (0,)))
    ).astype(BF)


def extra_rows(values, width):
    n = values.shape[1]
    hi = values.astype(BF).astype(F32)
    lo = (values - hi).astype(BF).astype(F32)
    row = lax.broadcasted_iota(jnp.int32, (EXTRA, n), 0)
    head = jnp.where(row == 0, hi, jnp.where(row == 1, lo, 0.0))
    return jnp.concatenate([head, jnp.zeros((EXTRA, width - n), F32)], axis=1).astype(BF)


def split_cores(core, total, summed, keep, keep_loss, give):
    rows = keep.shape[0]
    at = pl.multiple_of(core * rows, rows)
    away = pl.multiple_of((1 - core) * rows, rows)
    keep[...] = total[pl.ds(at, rows), :]
    give[:rows, :] = total[pl.ds(away, rows), :].astype(BF)
    zero, one = summed[:, :rows], summed[:, rows:]
    keep_loss[...] = jnp.where(core == 0, zero, one)
    give[rows:, :] = extra_rows(jnp.where(core == 0, one, zero), give.shape[1])


def visit_kernel(
    place, factors, mine, theirs, own, cross, far, near, first_slopes, first_loss, my_loss,
    slopes, far_slopes, loss, keep, keep_loss, give, total, first, second, their_loss,
):
    lay((own, cross), first)
    lay((far, near), second)
    slopes_and_loss(None, factors, theirs, second, slopes, their_loss)
    slopes_and_loss(None, factors, mine, far, far_slopes, loss)
    loss[...] += my_loss[...]
    total[...] = contract(first_slopes[...], first[...], ((0,), (0,))) + contract(
        slopes[...], second[...], ((0,), (0,))
    )
    split_cores(place[0], total, their_loss[...] + first_loss[...], keep, keep_loss, give)


def rest_kernel(
    place, mine, theirs, own, cross, far, near, my_slopes, far_slopes, first_slopes, slopes, loss, after,
    own_grad, far_grad, near_grad, keep, keep_loss, give, total, bundle,
):
    rows = own.shape[0]

    def text_gradient(of_mine, of_theirs):
        return contract(of_mine, mine[...], ((1,), (0,))) + contract(of_theirs, theirs[...], ((1,), (0,)))

    own_grad[...] = text_gradient(my_slopes[:rows, :], first_slopes[:rows, :])
    far_grad[...] = text_gradient(far_slopes[...], slopes[:rows, :]).astype(BF)
    near_grad[...] = text_gradient(my_slopes[2 * rows :, :], slopes[rows:, :]).astype(BF)
    lay((own, cross, near), bundle)
    total[...] = contract(my_slopes[...], bundle[...], ((0,), (0,))) + contract(
        far_slopes[...], far[...], ((0,), (0,))
    )
    split_cores(place[0], total, loss[...], keep, keep_loss, give)


def take(place, gathered, rows):
    size = rows + EXTRA
    at = pl.multiple_of((1 - place[0]) * size, size)
    got = gathered[pl.ds(at, rows), :].astype(F32)
    extra = gathered[pl.ds(pl.multiple_of(at + rows, EXTRA), EXTRA), :].astype(F32)
    return got, extra[0:1, :rows] + extra[1:2, :rows]


def visitor_kernel(place, keep, keep_loss, gathered, message):
    rows = keep.shape[0]
    got, got_loss = take(place, gathered, rows)
    message[:rows, :] = (keep[...] + got).astype(BF)
    message[rows:, :] = extra_rows(keep_loss[...] + got_loss, keep.shape[1])


def image_kernel(place, keep, keep_loss, gathered, home, grad, loss):
    rows = keep.shape[0]
    got, got_loss = take(place, gathered, rows)
    grad[...] = keep[...] + got + home[:rows, :].astype(F32)
    extra = home[rows:, :].astype(F32)
    loss[...] = (keep_loss[...] + got_loss + extra[0:1, :rows] + extra[1:2, :rows]) * (1.0 / (16 * rows))


SMEM = pl.BlockSpec(memory_space=pltpu.SMEM)
VMEM = pl.BlockSpec(memory_space=pltpu.VMEM)


def call(kernel, scalars, outs, scratch=()):
    def run(*args):
        return pl.pallas_call(
            kernel,
            out_shape=outs,
            in_specs=[SMEM] * scalars + [VMEM] * (len(args) - scalars),
            out_specs=[VMEM] * len(outs),
            scratch_shapes=list(scratch),
            compiler_params=pltpu.CompilerParams(vmem_limit_bytes=32 * 1024 * 1024),
            cost_estimate=pl.CostEstimate(flops=0, bytes_accessed=0, transcendentals=0),
        )(*args)

    return run


def solution(mesh):
    sizes = (4, 2, 4, 8, 2)
    fine = Mesh(mesh.devices.reshape(sizes), AXES)
    go = visit(sizes)
    back = [(b, a) for a, b in go]
    bar = lax.optimization_barrier
    across = [along_line(sizes, m) for m in range(sizes[0])]

    def shards(images, texts, scale, shift):
        rows, width = images.shape
        shape = jax.ShapeDtypeStruct
        place = lax.axis_index("c").reshape(1).astype(jnp.int32)
        factors = jnp.concatenate([scale, shift])
        block, wide = shape((rows, width), BF), shape((rows, width), F32)
        short, message = shape((1, rows), F32), shape((rows + EXTRA, width), BF)
        line = shape((1, 2 * rows), F32)
        total = pltpu.VMEM((2 * rows, width), F32)

        def slope(blocks):
            return shape((blocks * rows, 2 * rows), BF)

        def bundle(blocks):
            return pltpu.VMEM((blocks * rows, width), BF)

        def both_cores(array):
            return lax.all_gather(array, "c", axis=0, tiled=True)

        cross, near, far = (lax.ppermute(texts, AXES, across[m]) for m in (3, 1, 2))
        visitors = lax.ppermute(images, AXES, go)
        mine = both_cores(images)

        my_slopes, my_loss = call(own_kernel, 2, [slope(3), line], [bundle(3)])(
            place, factors, mine, texts, cross, near
        )
        visitors, my_slopes = bar((visitors, my_slopes))
        theirs = both_cores(visitors)
        slopes0, loss0, cross_grad = call(cross_kernel, 1, [slope(2), line, block], [bundle(2)])(
            factors, mine, theirs, texts, cross, my_slopes
        )
        cross_home = lax.ppermute(cross_grad, AXES, across[3])
        slopes1, far_slopes, loss, keep_v, keep_loss_v, give_v = call(
            visit_kernel,
            2,
            [slope(2), slope(1), line, wide, short, message],
            [total, bundle(2), bundle(2), pltpu.VMEM((1, 2 * rows), F32)],
        )(place, factors, mine, theirs, texts, cross, far, near, slopes0, loss0, my_loss)
        (sent,) = call(visitor_kernel, 1, [message])(place, keep_v, keep_loss_v, both_cores(give_v))
        home = lax.ppermute(sent, AXES, back)
        own_grad, far_grad, near_grad, keep, keep_loss, give = call(
            rest_kernel, 1, [wide, block, block, wide, short, message], [total, bundle(3)]
        )(place, mine, theirs, texts, cross, far, near, my_slopes, far_slopes, slopes0, slopes1, loss, sent)
        far_home = lax.ppermute(far_grad, AXES, across[2])
        near_home = lax.ppermute(near_grad, AXES, across[1])

        two = own_grad + cross_home.astype(F32)
        keep, two = bar((keep, two))
        grad_images, row_loss = call(image_kernel, 1, [wide, short])(
            place, keep, keep_loss, both_cores(give), home
        )
        grad_images, row_loss, two = bar((grad_images, row_loss, two))
        grad_texts = two + (far_home.astype(F32) + near_home.astype(F32))
        row_loss = row_loss.reshape(rows)
        return grad_images, grad_texts, row_loss

    whole = P(AXES, None)
    return jax.shard_map(
        shards,
        mesh=fine,
        in_specs=(whole, whole, P(), P()),
        out_specs=(whole, whole, P(AXES)),
        check_vma=False,
    )
```

```python
import functools

import jax
import jax.numpy as jnp
import numpy as np
from jax import lax
from jax.experimental import pallas as pl
from jax.experimental.pallas import tpu as pltpu
from jax.sharding import Mesh, PartitionSpec as P

AXES = ("yl", "c", "x", "z", "yh")
BF = jnp.bfloat16
F32 = jnp.float32
EXTRA = 16


def pairs(sizes, fn):
    out = []
    for src in np.ndindex(*sizes):
        out.append((int(np.ravel_multi_index(src, sizes)), int(np.ravel_multi_index(fn(*src), sizes))))
    return out


def visit(sizes):
    nyl, _, nx, nz, _ = sizes

    def fn(yl, c, x, z, yh):
        if yh == 1:
            return yl ^ 2, c, x, z, 0
        k = (x * nz + z - 1) % (nx * nz)
        return yl ^ 2, c, k // nz, k % nz, 1

    return pairs(sizes, fn)


def along_line(sizes, m):
    return pairs(sizes, lambda yl, c, x, z, yh: (yl ^ m, c, x, z, yh))


def contract(left, right, dims):
    return lax.dot_general(left, right, (dims, ((), ())), preferred_element_type=F32)


def slopes_and_loss(positive, factors, images, texts, slopes, loss):
    s, b = factors[0], factors[1]
    z = s * contract(texts[...], images[...], ((1,), (1,))) + b
    pair = positive(z.shape) if positive else None
    u = z if pair is None else jnp.where(pair, -z, z)
    e = jnp.exp(-jnp.abs(u))
    loss[...] = jnp.sum(jnp.maximum(u, 0.0) + jnp.log1p(e), axis=0, keepdims=True)
    slope = s * jnp.where(u >= 0, 1.0, e) / (1.0 + e)
    slopes[...] = (slope if pair is None else jnp.where(pair, -slope, slope)).astype(BF)


def lay(blocks, bundle):
    rows = blocks[0].shape[0]
    for m, block in enumerate(blocks):
        bundle[m * rows : (m + 1) * rows, :] = block[...]


def own_kernel(place, factors, mine, own, cross, slopes, loss, bundle):
    lay((own, cross), bundle)
    rows = own.shape[0]

    def positive(shape):
        i = lax.broadcasted_iota(jnp.int32, shape, 1) - place[0] * rows
        j = lax.broadcasted_iota(jnp.int32, shape, 0)
        return (i == j) & (j < rows)

    slopes_and_loss(positive, factors, mine, bundle, slopes, loss)


def cross_kernel(factors, mine, theirs, own, cross, my_slopes, slopes, loss, cross_grad, bundle):
    lay((own, cross), bundle)
    slopes_and_loss(None, factors, theirs, bundle, slopes, loss)
    rows = own.shape[0]
    cross_grad[...] = (
        contract(my_slopes[rows : 2 * rows, :], mine[...], ((1,), (0,)))
        + contract(slopes[rows:, :], theirs[...], ((1,), (0,)))
    ).astype(BF)


def extra_rows(values, width):
    n = values.shape[1]
    hi = values.astype(BF).astype(F32)
    lo = (values - hi).astype(BF).astype(F32)
    row = lax.broadcasted_iota(jnp.int32, (EXTRA, n), 0)
    head = jnp.where(row == 0, hi, jnp.where(row == 1, lo, 0.0))
    return jnp.concatenate([head, jnp.zeros((EXTRA, width - n), F32)], axis=1).astype(BF)


def split_cores(core, total, summed, keep, keep_loss, give):
    rows = keep.shape[0]
    at = pl.multiple_of(core * rows, rows)
    away = pl.multiple_of((1 - core) * rows, rows)
    keep[...] = total[pl.ds(at, rows), :]
    give[:rows, :] = total[pl.ds(away, rows), :].astype(BF)
    zero, one = summed[:, :rows], summed[:, rows:]
    keep_loss[...] = jnp.where(core == 0, zero, one)
    give[rows:, :] = extra_rows(jnp.where(core == 0, one, zero), give.shape[1])


def visit_kernel(
    place, factors, mine, theirs, own, cross, far, near, first_slopes, first_loss, my_loss,
    slopes, last_slopes, loss, keep, keep_loss, give, total, first, second, their_loss,
):
    lay((own, cross), first)
    lay((far, near), second)
    slopes_and_loss(None, factors, theirs, second, slopes, their_loss)
    slopes_and_loss(None, factors, mine, second, last_slopes, loss)
    loss[...] += my_loss[...]
    total[...] = contract(first_slopes[...], first[...], ((0,), (0,))) + contract(
        slopes[...], second[...], ((0,), (0,))
    )
    split_cores(place[0], total, their_loss[...] + first_loss[...], keep, keep_loss, give)


def rest_kernel(
    place, mine, theirs, own, cross, far, near, my_slopes, last_slopes, first_slopes, slopes, loss, after,
    own_grad, far_grad, near_grad, keep, keep_loss, give, total, first, second,
):
    rows = own.shape[0]

    def text_gradient(of_mine, of_theirs):
        return contract(of_mine, mine[...], ((1,), (0,))) + contract(of_theirs, theirs[...], ((1,), (0,)))

    own_grad[...] = text_gradient(my_slopes[:rows, :], first_slopes[:rows, :])
    far_grad[...] = text_gradient(last_slopes[:rows, :], slopes[:rows, :]).astype(BF)
    near_grad[...] = text_gradient(last_slopes[rows:, :], slopes[rows:, :]).astype(BF)
    lay((own, cross), first)
    lay((far, near), second)
    total[...] = contract(my_slopes[...], first[...], ((0,), (0,))) + contract(
        last_slopes[...], second[...], ((0,), (0,))
    )
    split_cores(place[0], total, loss[...], keep, keep_loss, give)


def take(place, gathered, rows):
    size = rows + EXTRA
    at = pl.multiple_of((1 - place[0]) * size, size)
    got = gathered[pl.ds(at, rows), :].astype(F32)
    extra = gathered[pl.ds(pl.multiple_of(at + rows, EXTRA), EXTRA), :].astype(F32)
    return got, extra[0:1, :rows] + extra[1:2, :rows]


def visitor_kernel(place, keep, keep_loss, gathered, message):
    rows = keep.shape[0]
    got, got_loss = take(place, gathered, rows)
    message[:rows, :] = (keep[...] + got).astype(BF)
    message[rows:, :] = extra_rows(keep_loss[...] + got_loss, keep.shape[1])


def image_kernel(place, keep, keep_loss, gathered, home, grad, loss):
    rows = keep.shape[0]
    got, got_loss = take(place, gathered, rows)
    grad[...] = keep[...] + got + home[:rows, :].astype(F32)
    extra = home[rows:, :].astype(F32)
    loss[...] = (keep_loss[...] + got_loss + extra[0:1, :rows] + extra[1:2, :rows]) * (1.0 / (16 * rows))


SMEM = pl.BlockSpec(memory_space=pltpu.SMEM)
VMEM = pl.BlockSpec(memory_space=pltpu.VMEM)


def call(kernel, scalars, outs, scratch=()):
    def run(*args):
        return pl.pallas_call(
            kernel,
            out_shape=outs,
            in_specs=[SMEM] * scalars + [VMEM] * (len(args) - scalars),
            out_specs=[VMEM] * len(outs),
            scratch_shapes=list(scratch),
            compiler_params=pltpu.CompilerParams(vmem_limit_bytes=32 * 1024 * 1024),
            cost_estimate=pl.CostEstimate(flops=0, bytes_accessed=0, transcendentals=0),
        )(*args)

    return run


def solution(mesh):
    sizes = (4, 2, 4, 8, 2)
    fine = Mesh(mesh.devices.reshape(sizes), AXES)
    go = visit(sizes)
    back = [(b, a) for a, b in go]
    bar = lax.optimization_barrier
    across = [along_line(sizes, m) for m in range(sizes[0])]

    def shards(images, texts, scale, shift):
        rows, width = images.shape
        shape = jax.ShapeDtypeStruct
        place = lax.axis_index("c").reshape(1).astype(jnp.int32)
        factors = jnp.concatenate([scale, shift])
        block, wide = shape((rows, width), BF), shape((rows, width), F32)
        short, message = shape((1, rows), F32), shape((rows + EXTRA, width), BF)
        line = shape((1, 2 * rows), F32)
        total = pltpu.VMEM((2 * rows, width), F32)

        def slope(blocks):
            return shape((blocks * rows, 2 * rows), BF)

        def bundle(blocks):
            return pltpu.VMEM((blocks * rows, width), BF)

        def both_cores(array):
            return lax.all_gather(array, "c", axis=0, tiled=True)

        cross, near, far = (lax.ppermute(texts, AXES, across[m]) for m in (3, 1, 2))
        visitors = lax.ppermute(images, AXES, go)
        mine = both_cores(images)

        my_slopes, my_loss = call(own_kernel, 2, [slope(2), line], [bundle(2)])(
            place, factors, mine, texts, cross
        )
        visitors, my_slopes = bar((visitors, my_slopes))
        theirs = both_cores(visitors)
        slopes0, loss0, cross_grad = call(cross_kernel, 1, [slope(2), line, block], [bundle(2)])(
            factors, mine, theirs, texts, cross, my_slopes
        )
        cross_home = lax.ppermute(cross_grad, AXES, across[3])
        slopes1, last_slopes, loss, keep_v, keep_loss_v, give_v = call(
            visit_kernel,
            2,
            [slope(2), slope(2), line, wide, short, message],
            [total, bundle(2), bundle(2), pltpu.VMEM((1, 2 * rows), F32)],
        )(place, factors, mine, theirs, texts, cross, far, near, slopes0, loss0, my_loss)
        (sent,) = call(visitor_kernel, 1, [message])(place, keep_v, keep_loss_v, both_cores(give_v))
        home = lax.ppermute(sent, AXES, back)
        own_grad, far_grad, near_grad, keep, keep_loss, give = call(
            rest_kernel, 1, [wide, block, block, wide, short, message], [total, bundle(2), bundle(2)]
        )(place, mine, theirs, texts, cross, far, near, my_slopes, last_slopes, slopes0, slopes1, loss, sent)
        far_home = lax.ppermute(far_grad, AXES, across[2])
        near_home = lax.ppermute(near_grad, AXES, across[1])

        two = own_grad + cross_home.astype(F32)
        keep, two = bar((keep, two))
        grad_images, row_loss = call(image_kernel, 1, [wide, short])(
            place, keep, keep_loss, both_cores(give), home
        )
        grad_images, row_loss, two = bar((grad_images, row_loss, two))
        grad_texts = two + (far_home.astype(F32) + near_home.astype(F32))
        row_loss = row_loss.reshape(rows)
        return grad_images, grad_texts, row_loss

    whole = P(AXES, None)
    return jax.shard_map(
        shards,
        mesh=fine,
        in_specs=(whole, whole, P(), P()),
        out_specs=(whole, whole, P(AXES)),
        check_vma=False,
    )
```

```python
import functools

import jax
import jax.numpy as jnp
import numpy as np
from jax import lax
from jax.experimental import pallas as pl
from jax.experimental.pallas import tpu as pltpu
from jax.sharding import Mesh, PartitionSpec as P

AXES = ("yl", "c", "x", "z", "yh")
BF = jnp.bfloat16
F32 = jnp.float32
EXTRA = 16


def pairs(sizes, fn):
    out = []
    for src in np.ndindex(*sizes):
        out.append((int(np.ravel_multi_index(src, sizes)), int(np.ravel_multi_index(fn(*src), sizes))))
    return out


def visit(sizes):
    nyl, _, nx, nz, _ = sizes

    def fn(yl, c, x, z, yh):
        if yh == 1:
            return yl ^ 2, c, x, z, 0
        k = (x * nz + z - 1) % (nx * nz)
        return yl ^ 2, c, k // nz, k % nz, 1

    return pairs(sizes, fn)


def along_line(sizes, m):
    return pairs(sizes, lambda yl, c, x, z, yh: (yl ^ m, c, x, z, yh))


def contract(left, right, dims):
    return lax.dot_general(left, right, (dims, ((), ())), preferred_element_type=F32)


def slopes_and_loss(positive, factors, images, texts, slopes, loss):
    s, b = factors[0], factors[1]
    z = s * contract(texts[...], images[...], ((1,), (1,))) + b
    pair = positive(z.shape) if positive else None
    u = z if pair is None else jnp.where(pair, -z, z)
    e = jnp.exp(-jnp.abs(u))
    loss[...] = jnp.sum(jnp.maximum(u, 0.0) + jnp.log1p(e), axis=0, keepdims=True)
    slope = s * jnp.where(u >= 0, 1.0, e) / (1.0 + e)
    slopes[...] = (slope if pair is None else jnp.where(pair, -slope, slope)).astype(BF)


def lay(blocks, bundle):
    rows = blocks[0].shape[0]
    for m, block in enumerate(blocks):
        bundle[m * rows : (m + 1) * rows, :] = block[...]


def own_kernel(place, factors, mine, own, cross, slopes, loss, bundle):
    lay((own, cross), bundle)
    rows = own.shape[0]

    def positive(shape):
        i = lax.broadcasted_iota(jnp.int32, shape, 1) - place[0] * rows
        j = lax.broadcasted_iota(jnp.int32, shape, 0)
        return (i == j) & (j < rows)

    slopes_and_loss(positive, factors, mine, bundle, slopes, loss)


def cross_kernel(factors, mine, theirs, own, cross, my_slopes, slopes, loss, cross_grad, bundle):
    lay((own, cross), bundle)
    slopes_and_loss(None, factors, theirs, bundle, slopes, loss)
    rows = own.shape[0]
    cross_grad[...] = (
        contract(my_slopes[rows : 2 * rows, :], mine[...], ((1,), (0,)))
        + contract(slopes[rows:, :], theirs[...], ((1,), (0,)))
    ).astype(BF)


def extra_rows(values, width):
    n = values.shape[1]
    hi = values.astype(BF).astype(F32)
    lo = (values - hi).astype(BF).astype(F32)
    row = lax.broadcasted_iota(jnp.int32, (EXTRA, n), 0)
    head = jnp.where(row == 0, hi, jnp.where(row == 1, lo, 0.0))
    return jnp.concatenate([head, jnp.zeros((EXTRA, width - n), F32)], axis=1).astype(BF)


def split_cores(core, total, summed, keep, keep_loss, give):
    rows = keep.shape[0]
    at = pl.multiple_of(core * rows, rows)
    away = pl.multiple_of((1 - core) * rows, rows)
    keep[...] = total[pl.ds(at, rows), :]
    give[:rows, :] = total[pl.ds(away, rows), :].astype(BF)
    zero, one = summed[:, :rows], summed[:, rows:]
    keep_loss[...] = jnp.where(core == 0, zero, one)
    give[rows:, :] = extra_rows(jnp.where(core == 0, one, zero), give.shape[1])


def visit_kernel(
    place, factors, mine, theirs, own, cross, far, near, first_slopes, first_loss, my_loss,
    slopes, last_slopes, loss, keep, keep_loss, give, total, first, second, their_loss,
):
    lay((own, cross), first)
    lay((far, near), second)
    slopes_and_loss(None, factors, theirs, second, slopes, their_loss)
    slopes_and_loss(None, factors, mine, second, last_slopes, loss)
    loss[...] += my_loss[...]
    total[...] = contract(first_slopes[...], first[...], ((0,), (0,))) + contract(
        slopes[...], second[...], ((0,), (0,))
    )
    split_cores(place[0], total, their_loss[...] + first_loss[...], keep, keep_loss, give)


def text_kernel(mine, theirs, last_slopes, slopes, after, far_grad, near_grad):
    rows = far_grad.shape[0]
    grad = contract(last_slopes[...], mine[...], ((1,), (0,))) + contract(slopes[...], theirs[...], ((1,), (0,)))
    far_grad[...] = grad[:rows, :].astype(BF)
    near_grad[...] = grad[rows:, :].astype(BF)


def rest_kernel(
    place, mine, theirs, own, cross, far, near, my_slopes, last_slopes, first_slopes, loss, after,
    own_grad, keep, keep_loss, give, total, first, second,
):
    rows = own.shape[0]
    own_grad[...] = contract(my_slopes[:rows, :], mine[...], ((1,), (0,))) + contract(
        first_slopes[:rows, :], theirs[...], ((1,), (0,))
    )
    lay((own, cross), first)
    lay((far, near), second)
    total[...] = contract(my_slopes[...], first[...], ((0,), (0,))) + contract(
        last_slopes[...], second[...], ((0,), (0,))
    )
    split_cores(place[0], total, loss[...], keep, keep_loss, give)


def take(place, gathered, rows):
    size = rows + EXTRA
    at = pl.multiple_of((1 - place[0]) * size, size)
    got = gathered[pl.ds(at, rows), :].astype(F32)
    extra = gathered[pl.ds(pl.multiple_of(at + rows, EXTRA), EXTRA), :].astype(F32)
    return got, extra[0:1, :rows] + extra[1:2, :rows]


def visitor_kernel(place, keep, keep_loss, gathered, message):
    rows = keep.shape[0]
    got, got_loss = take(place, gathered, rows)
    message[:rows, :] = (keep[...] + got).astype(BF)
    message[rows:, :] = extra_rows(keep_loss[...] + got_loss, keep.shape[1])


def image_kernel(place, keep, keep_loss, gathered, home, grad, loss):
    rows = keep.shape[0]
    got, got_loss = take(place, gathered, rows)
    grad[...] = keep[...] + got + home[:rows, :].astype(F32)
    extra = home[rows:, :].astype(F32)
    loss[...] = (keep_loss[...] + got_loss + extra[0:1, :rows] + extra[1:2, :rows]) * (1.0 / (16 * rows))


SMEM = pl.BlockSpec(memory_space=pltpu.SMEM)
VMEM = pl.BlockSpec(memory_space=pltpu.VMEM)


def call(kernel, scalars, outs, scratch=()):
    def run(*args):
        return pl.pallas_call(
            kernel,
            out_shape=outs,
            in_specs=[SMEM] * scalars + [VMEM] * (len(args) - scalars),
            out_specs=[VMEM] * len(outs),
            scratch_shapes=list(scratch),
            compiler_params=pltpu.CompilerParams(vmem_limit_bytes=32 * 1024 * 1024),
            cost_estimate=pl.CostEstimate(flops=0, bytes_accessed=0, transcendentals=0),
        )(*args)

    return run


def solution(mesh):
    sizes = (4, 2, 4, 8, 2)
    fine = Mesh(mesh.devices.reshape(sizes), AXES)
    go = visit(sizes)
    back = [(b, a) for a, b in go]
    bar = lax.optimization_barrier
    across = [along_line(sizes, m) for m in range(sizes[0])]

    def shards(images, texts, scale, shift):
        rows, width = images.shape
        shape = jax.ShapeDtypeStruct
        place = lax.axis_index("c").reshape(1).astype(jnp.int32)
        factors = jnp.concatenate([scale, shift])
        block, wide = shape((rows, width), BF), shape((rows, width), F32)
        short, message = shape((1, rows), F32), shape((rows + EXTRA, width), BF)
        line = shape((1, 2 * rows), F32)
        total = pltpu.VMEM((2 * rows, width), F32)

        def slope(blocks):
            return shape((blocks * rows, 2 * rows), BF)

        def bundle(blocks):
            return pltpu.VMEM((blocks * rows, width), BF)

        def both_cores(array):
            return lax.all_gather(array, "c", axis=0, tiled=True)

        cross, near, far = (lax.ppermute(texts, AXES, across[m]) for m in (3, 1, 2))
        visitors = lax.ppermute(images, AXES, go)
        mine = both_cores(images)

        my_slopes, my_loss = call(own_kernel, 2, [slope(2), line], [bundle(2)])(
            place, factors, mine, texts, cross
        )
        visitors, my_slopes = bar((visitors, my_slopes))
        theirs = both_cores(visitors)
        slopes0, loss0, cross_grad = call(cross_kernel, 1, [slope(2), line, block], [bundle(2)])(
            factors, mine, theirs, texts, cross, my_slopes
        )
        cross_home = lax.ppermute(cross_grad, AXES, across[3])
        slopes1, last_slopes, loss, keep_v, keep_loss_v, give_v = call(
            visit_kernel,
            2,
            [slope(2), slope(2), line, wide, short, message],
            [total, bundle(2), bundle(2), pltpu.VMEM((1, 2 * rows), F32)],
        )(place, factors, mine, theirs, texts, cross, far, near, slopes0, loss0, my_loss)
        (sent,) = call(visitor_kernel, 1, [message])(place, keep_v, keep_loss_v, both_cores(give_v))
        home = lax.ppermute(sent, AXES, back)
        far_grad, near_grad = call(text_kernel, 0, [block, block])(mine, theirs, last_slopes, slopes1, sent)
        far_home = lax.ppermute(far_grad, AXES, across[2])
        near_home = lax.ppermute(near_grad, AXES, across[1])
        own_grad, keep, keep_loss, give = call(
            rest_kernel, 1, [wide, wide, short, message], [total, bundle(2), bundle(2)]
        )(place, mine, theirs, texts, cross, far, near, my_slopes, last_slopes, slopes0, loss, near_grad)

        two = own_grad + cross_home.astype(F32)
        keep, two = bar((keep, two))
        grad_images, row_loss = call(image_kernel, 1, [wide, short])(
            place, keep, keep_loss, both_cores(give), home
        )
        grad_images, row_loss, two = bar((grad_images, row_loss, two))
        grad_texts = two + (far_home.astype(F32) + near_home.astype(F32))
        row_loss = row_loss.reshape(rows)
        return grad_images, grad_texts, row_loss

    whole = P(AXES, None)
    return jax.shard_map(
        shards,
        mesh=fine,
        in_specs=(whole, whole, P(), P()),
        out_specs=(whole, whole, P(AXES)),
        check_vma=False,
    )
```
